32 devices in a mesh: groups: 2 (over x), band: 8 (over z, y), sub: 2 (over core).
Axes of the slice: x: 2, y: 2, z: 4, core: 2. Of those that a mesh axis runs over, the one named last changes fastest.
Arguments:
- state: bfloat16 [154, 96, 240], P('groups', 'band', 'sub'), parts along dimension 0, may hold values from -6 to 6
- target: bfloat16 [154, 96, 240], P('groups', 'band', 'sub'), parts along dimension 0, may hold values from -6 to 6
- tile_plan: int32 [16, 20], P('groups'), parts along dimension 0, may hold values from -1 to 31, as said below
- w_enc: bfloat16 [77, 256], replicated, may hold values from -0.625 to 0.625
- dw_kernel: bfloat16 [49, 256], replicated, may hold values from -0.875 to 0.875
- norm_gain: float32 [256], replicated, may hold values from 0.1 to 1.9
- w_up: bfloat16 [256, 1024], replicated, may hold values from -0.375 to 0.375
- w_down: bfloat16 [1024, 256], replicated, may hold values from -0.1875 to 0.1875
- w_dec: bfloat16 [256, 77], replicated, may hold values from -0.375 to 0.375
Outputs:
- predicted_state: bfloat16 [154, 96, 240], P('groups', 'band', 'sub'), parts along dimension 0
- loss: float32 [2], P('groups'), parts along dimension 0
- grad_w_enc: float32 [154, 256], P('groups'), parts along dimension 0
- grad_dw_kernel: float32 [98, 256], P('groups'), parts along dimension 0
- grad_norm_gain: float32 [512], P('groups'), parts along dimension 0
- grad_w_up: float32 [512, 1024], P('groups'), parts along dimension 0
- grad_w_down: float32 [2048, 256], P('groups'), parts along dimension 0
- grad_w_dec: float32 [512, 77], P('groups'), parts along dimension 0
The draws below stay inside these ranges and needn't reach their ends.
There are 2 independent parts, one for each index of `groups`. The reference program is written for one: setup_inputs(seed, part) draws one part's arguments, and reference() takes and returns one part's arrays. A program takes and returns all parts, laid end to end along the dimension named above; an argument that names none is the same for every part. Nothing has to cross between parts.
Inputs may be any that keep to these rules, and one draw needn't show every extreme that they name: `tile_plan`: for a wet tile held by band index e in one half of sub, the value d * 4 + s names band index d and slot s of a computing device in the same half of sub, where d - e taken cyclically over the band indices lies between -2 and 2. In each half of sub every slot of every band index is named by exactly one wet tile. Wet tiles come in pairs of longitude neighbours (tile columns 2m and 2m+1 of one device's 10 columns) that go to one device in slots 2k and 2k+1, and one device holds at most one such pair for one computing band, so at most 2 tiles; every draw reaches that.
All inputs are finite; a program needn't handle non-finite values.
Results may differ from the reference program's by a relative error of at most 0.0042.
Values may be sent and summed in bfloat16 or wider, within the bound.
A program may use at most 64 MiB of HBM per device.

```python
import math
import jax
import jax.numpy as jnp
import numpy as np
from jax import lax

C = 77
W = 256
HID = 1024
KSIZE = 7
PATCH_WIDTH = 12
TR = 1
TC = 10
TILES_CMP = 4
REACH = 2
ROWS_T = 8
ROWS = 96
COLS = 240
N_BAND = 8
N_SUB = 2


def column_plan(key):
    band_total = ROWS_T // TR
    pair_count = TR * TC // 2
    reach_span = 2 * REACH + 1
    half_slots = TILES_CMP // 2
    key_offset, key_position = jax.random.split(key, 2)
    offset_score = jax.random.randint(key_offset, (band_total, reach_span), 0, 1024) * reach_span
    offset_score = offset_score + jnp.arange(reach_span, dtype=jnp.int32)[None, :]
    chosen = jnp.argsort(offset_score, axis=1)[:, :half_slots].astype(jnp.int32)
    position_score = jax.random.randint(key_position, (band_total, pair_count), 0, 1024) * pair_count
    position_score = position_score + jnp.arange(pair_count, dtype=jnp.int32)[None, :]
    position_of = jnp.argsort(position_score, axis=1)[:, :reach_span].astype(jnp.int32)
    dest_band = jnp.arange(band_total, dtype=jnp.int32)[:, None]
    source_band = (dest_band - (chosen - REACH)) % band_total
    position = position_of[source_band, chosen]
    first_value = dest_band * TILES_CMP + 2 * jnp.arange(half_slots, dtype=jnp.int32)[None, :]
    first_tile = jnp.full((band_total, pair_count), -1, jnp.int32).at[source_band, position].set(first_value)
    second_tile = jnp.where(first_tile >= 0, first_tile + 1, -1)
    first_tile = first_tile.reshape(band_total, TR, TC // 2)
    second_tile = second_tile.reshape(band_total, TR, TC // 2)
    tile_values = jnp.stack([first_tile, second_tile], axis=-1).reshape(band_total * TR, TC)
    return tile_values.astype(jnp.int32)


def draw_tile_plan(key, part):
    west_half = column_plan(jax.random.fold_in(key, 11))
    east_half = column_plan(jax.random.fold_in(key, 12))
    return jnp.concatenate([west_half, east_half], axis=1)


def steps_of(rng, extent, shards, smallest, high):
    def one(dim, parts):
        heights = jax.random.uniform(jax.random.fold_in(jax.random.fold_in(rng, 6), dim), (parts,), jnp.float32, smallest / len(shards), high / len(shards))
        return jnp.repeat(jnp.exp(heights), extent[dim] // parts).reshape((-1,) + (1,) * (len(extent) - dim - 1))

    factor_of = one(*shards[0])
    for cut in shards[1:]:
        factor_of = factor_of * one(*cut)
    return factor_of


def normal_values(key, shape, scale, limit, cuts=(), held_as=jnp.bfloat16):
    array = scale * jax.random.normal(key, shape, jnp.float32)
    if cuts:
        array = array * steps_of(key, shape, cuts, -0.22, 0.18)
    return jnp.clip(array, -limit, limit).astype(held_as)


def setup_inputs(seed: int = 0, part: int = 0) -> dict:
    keys = jax.random.split(jax.random.key(seed), 10)
    own_keys = jax.random.split(jax.random.fold_in(keys[9], part), 10)
    state = normal_values(own_keys[0], (C, ROWS, COLS), 1.0, 6.0, ((1, 8), (2, 2)))
    target = normal_values(own_keys[1], (C, ROWS, COLS), 1.0, 6.0, ((1, 8), (2, 2)))
    tile_plan = draw_tile_plan(jax.random.fold_in(jax.random.fold_in(keys[9], part), 71), part)
    w_enc = normal_values(keys[3], (C, W), C ** -0.5, 0.625)
    dw_kernel = normal_values(keys[4], (KSIZE * KSIZE, W), (KSIZE * KSIZE) ** -0.5, 0.875)
    norm_gain = jnp.clip(1.0 + 0.18 * jax.random.normal(keys[5], (W,), jnp.float32), 0.1, 1.9)
    w_up = normal_values(keys[6], (W, HID), W ** -0.5, 0.375)
    w_down = normal_values(keys[7], (HID, W), HID ** -0.5, 0.1875)
    w_dec = normal_values(keys[8], (W, C), W ** -0.5, 0.375)
    return {"state": state, "target": target, "tile_plan": tile_plan, "w_enc": w_enc, "dw_kernel": dw_kernel, "norm_gain": norm_gain, "w_up": w_up, "w_down": w_down, "w_dec": w_dec}


def contract(form, left, right):
    return jnp.einsum(form, left.astype(jnp.float32), right.astype(jnp.float32))

def tile_terms(tiles_in, desired_patches, ocean_indicator, reciprocal_cells, w_enc, dw_kernel, norm_gain, w_up, w_down, w_dec):
    patch_identifier = tiles_in.shape[0]
    feature_depth = tiles_in.shape[1]
    hidden_width = w_enc.shape[1]
    tile_edge = PATCH_WIDTH + KSIZE - 1
    rim_cells = KSIZE // 2
    encoded = contract('bcp,cw->bpw', tiles_in, w_enc).astype(jnp.bfloat16)
    encoded = encoded.reshape(patch_identifier, tile_edge, tile_edge, hidden_width)
    kernel = dw_kernel.astype(jnp.float32)
    mixed_conv = jnp.zeros((patch_identifier, PATCH_WIDTH, PATCH_WIDTH, hidden_width), jnp.float32)
    for offset in range(KSIZE * KSIZE):
        row_shift, col_shift = divmod(offset, KSIZE)
        window = encoded[:, row_shift:row_shift + PATCH_WIDTH, col_shift:col_shift + PATCH_WIDTH, :].astype(jnp.float32)
        mixed_conv = mixed_conv + window * kernel[offset]
    centre_mean = lax.optimization_barrier(jnp.mean(mixed_conv, axis=-1, keepdims=True))
    centred = mixed_conv - centre_mean
    variance = lax.optimization_barrier(jnp.mean(centred * centred, axis=-1, keepdims=True))
    inv_std = lax.rsqrt(variance + 1e-06)
    normed = centred * inv_std
    gain_vec = norm_gain.astype(jnp.float32)
    scaled = (normed * gain_vec).astype(jnp.bfloat16).reshape(-1, hidden_width)
    pre_act = jnp.dot(scaled, w_up, preferred_element_type=jnp.float32)
    activated = jax.nn.gelu(pre_act).astype(jnp.bfloat16)
    expanded = jnp.dot(activated, w_down, preferred_element_type=jnp.float32)
    centre = encoded[:, rim_cells:rim_cells + PATCH_WIDTH, rim_cells:rim_cells + PATCH_WIDTH, :].reshape(-1, hidden_width)
    residual = (centre.astype(jnp.float32) + expanded).astype(jnp.bfloat16)
    readout_result = jnp.dot(residual, w_dec, preferred_element_type=jnp.float32)
    readout_result = readout_result.reshape(patch_identifier, PATCH_WIDTH * PATCH_WIDTH, feature_depth).transpose(0, 2, 1)
    unchanged_baseline = tiles_in.reshape(patch_identifier, feature_depth, tile_edge, tile_edge)
    unchanged_baseline = unchanged_baseline[:, :, rim_cells:rim_cells + PATCH_WIDTH, rim_cells:rim_cells + PATCH_WIDTH]
    predicted_state = unchanged_baseline.reshape(patch_identifier, feature_depth, PATCH_WIDTH * PATCH_WIDTH).astype(jnp.float32) + readout_result
    prediction_misfit = (predicted_state - desired_patches.astype(jnp.float32)) * ocean_indicator[:, None, None]
    objective_sum = jnp.sum(prediction_misfit * prediction_misfit) * reciprocal_cells
    upstream_sensitivity = (prediction_misfit * (2.0 * reciprocal_cells)).transpose(0, 2, 1).reshape(-1, feature_depth).astype(jnp.bfloat16)
    readout_sensitivity = jnp.dot(residual.T, upstream_sensitivity, preferred_element_type=jnp.float32)
    grad_res = jnp.dot(upstream_sensitivity, w_dec.T, preferred_element_type=jnp.float32).astype(jnp.bfloat16)
    contracting_sensitivity = jnp.dot(activated.T, grad_res, preferred_element_type=jnp.float32)
    grad_act = jnp.dot(grad_res, w_down.T, preferred_element_type=jnp.float32)
    grad_pre = jax.vjp(jax.nn.gelu, pre_act)[1](grad_act)[0].astype(jnp.bfloat16)
    widening_sensitivity = jnp.dot(scaled.T, grad_pre, preferred_element_type=jnp.float32)
    grad_scaled = jnp.dot(grad_pre, w_up.T, preferred_element_type=jnp.float32)
    grad_scaled = grad_scaled.reshape(patch_identifier, PATCH_WIDTH, PATCH_WIDTH, hidden_width)
    norm_scale_sensitivity = lax.optimization_barrier(jnp.sum(grad_scaled * normed, axis=(0, 1, 2)))
    grad_normed = grad_scaled * gain_vec
    grad_conv = inv_std * (grad_normed - lax.optimization_barrier(jnp.mean(grad_normed, axis=-1, keepdims=True)) - normed * lax.optimization_barrier(jnp.mean(grad_normed * normed, axis=-1, keepdims=True)))
    grad_enc = jnp.zeros((patch_identifier, tile_edge, tile_edge, hidden_width), jnp.float32)
    grad_enc = grad_enc.at[:, rim_cells:rim_cells + PATCH_WIDTH, rim_cells:rim_cells + PATCH_WIDTH, :].add(grad_res.astype(jnp.float32).reshape(patch_identifier, PATCH_WIDTH, PATCH_WIDTH, hidden_width))
    kernel_rows = []
    for offset in range(KSIZE * KSIZE):
        row_shift, col_shift = divmod(offset, KSIZE)
        window = encoded[:, row_shift:row_shift + PATCH_WIDTH, col_shift:col_shift + PATCH_WIDTH, :].astype(jnp.float32)
        kernel_rows.append(lax.optimization_barrier(jnp.sum(grad_conv * window, axis=(0, 1, 2))))
        grad_enc = grad_enc.at[:, row_shift:row_shift + PATCH_WIDTH, col_shift:col_shift + PATCH_WIDTH, :].add(grad_conv * kernel[offset])
    stencil_sensitivity = jnp.stack(kernel_rows)
    grad_enc_b = grad_enc.astype(jnp.bfloat16).reshape(patch_identifier, tile_edge * tile_edge, hidden_width)
    entry_sensitivity = contract('bcp,bpw->cw', tiles_in, grad_enc_b)
    return (predicted_state, objective_sum, (entry_sensitivity, stencil_sensitivity, norm_scale_sensitivity, widening_sensitivity, contracting_sensitivity, readout_sensitivity))

def run_blocks(tiles_in, desired_patches, ocean_indicator, reciprocal_cells, weights):
    patch_identifier = tiles_in.shape[0]
    block_size = math.gcd(patch_identifier, 2)
    block_count = patch_identifier // block_size
    empty_grads = tuple((jnp.zeros(weight.shape, jnp.float32) for weight in weights))

    def one_block(running, pieces):
        predicted, objective_sum, gradients = tile_terms(pieces[0], pieces[1], pieces[2], reciprocal_cells, *weights)
        summed = tuple((first + second for first, second in zip(running[1], gradients)))
        return ((running[0] + objective_sum, summed), predicted)
    start = (jnp.zeros((), jnp.float32), empty_grads)
    pieces = (tiles_in.reshape((block_count, block_size) + tiles_in.shape[1:]), desired_patches.reshape((block_count, block_size) + desired_patches.shape[1:]), ocean_indicator.reshape(block_count, block_size))
    (objective_sum, gradients), predicted = lax.scan(one_block, start, pieces)
    return (predicted.reshape((patch_identifier,) + predicted.shape[2:]), objective_sum, gradients)

def reference(state, target, tile_plan, w_enc, dw_kernel, norm_gain, w_up, w_down, w_dec):
    feature_depth = state.shape[0]
    rim_cells = KSIZE // 2
    tile_edge = PATCH_WIDTH + KSIZE - 1
    tile_rows = state.shape[1] // PATCH_WIDTH
    tile_cols = state.shape[2] // PATCH_WIDTH
    total_tiles = tile_rows * tile_cols
    wet_total = N_BAND * N_SUB * TILES_CMP
    lon_wide = jnp.concatenate([state[:, :, -rim_cells:], state, state[:, :, :rim_cells]], axis=2)
    padded = jnp.pad(lon_wide, ((0, 0), (rim_cells, rim_cells), (0, 0)))
    row_index = np.arange(tile_rows)[:, None] * PATCH_WIDTH + np.arange(tile_edge)[None, :]
    col_index = np.arange(tile_cols)[:, None] * PATCH_WIDTH + np.arange(tile_edge)[None, :]
    picked = padded[:, row_index, :][:, :, :, col_index]
    tiles_in = picked.transpose(1, 3, 0, 2, 4).reshape(total_tiles, feature_depth, tile_edge * tile_edge)
    desired_patches = target.reshape(feature_depth, tile_rows, PATCH_WIDTH, tile_cols, PATCH_WIDTH).transpose(1, 3, 0, 2, 4)
    desired_patches = desired_patches.reshape(total_tiles, feature_depth, PATCH_WIDTH * PATCH_WIDTH)
    wet_tiles = tile_plan >= 0
    reciprocal_cells = 1.0 / (jnp.sum(wet_tiles.astype(jnp.float32)) * (feature_depth * PATCH_WIDTH * PATCH_WIDTH))
    flat_wet = wet_tiles.reshape(-1)
    order_key = jnp.where(flat_wet, 0, total_tiles).astype(jnp.int32) + jnp.arange(total_tiles, dtype=jnp.int32)
    chosen = jnp.argsort(order_key)[:wet_total].astype(jnp.int32)
    weights = (w_enc, dw_kernel, norm_gain, w_up, w_down, w_dec)
    predicted, objective_sum, gradients = run_blocks(tiles_in[chosen], desired_patches[chosen], flat_wet[chosen].astype(jnp.float32), reciprocal_cells, weights)
    placed = jnp.zeros((total_tiles, feature_depth, PATCH_WIDTH * PATCH_WIDTH), jnp.float32).at[chosen].set(predicted)
    tiles_out = placed.astype(jnp.bfloat16).reshape(tile_rows, tile_cols, feature_depth, PATCH_WIDTH, PATCH_WIDTH)
    tiles_out = tiles_out.transpose(2, 0, 3, 1, 4).reshape(feature_depth, tile_rows * PATCH_WIDTH, tile_cols * PATCH_WIDTH)
    wet_cells = jnp.repeat(jnp.repeat(wet_tiles, PATCH_WIDTH, axis=0), PATCH_WIDTH, axis=1)
    new_field = jnp.where(wet_cells[None], tiles_out, state)
    return (new_field, objective_sum.reshape(1), gradients[0], gradients[1], gradients[2], gradients[3], gradients[4], gradients[5])
```

```python
import functools
import math

import jax
import jax.numpy as jnp
from jax import lax
from jax.experimental import pallas as pl
from jax.experimental.pallas import tpu as pltpu
from jax.sharding import PartitionSpec as P

KSIZE = 7
RIM = 3
PW = 12
LANES = 128
F32 = jnp.float32
BF16 = jnp.bfloat16
GELU_C = math.sqrt(2.0 / math.pi)
GELU_A = 0.044715


def with_halo(value, axis, dim, width, wrap):
    size, length = (lax.axis_size(axis), value.shape[dim])
    up = [(i, (i + 1) % size) for i in range(size if wrap else size - 1)]
    down = [(j, i) for i, j in up]
    last = lax.slice_in_dim(value, length - width, length, axis=dim)
    leading = lax.slice_in_dim(value, 0, width, axis=dim)
    return lax.ppermute(last, axis, up), lax.ppermute(leading, axis, down)


def dot(left, right, dims):
    return lax.dot_general(left, right, ((dims[:1], dims[1:]), ((), ())), preferred_element_type=F32)


def block_kernel(
    x_ref, goal_ref, mask_ref, gscale_ref, w_enc_ref, dw_ref, gain_ref, w_up_ref, w_down_ref,
    w_dec_t_ref, pred_ref, pack_ref, shifted, conv, gres_all, taps, dk, up_acc, down_acc,
):
    chan = x_ref.shape[1]
    width = w_enc_ref.shape[1]
    hid = w_up_ref.shape[1]
    rows = goal_ref.shape[0]
    wide = rows + KSIZE - 1
    groups = (LANES - 8) // 8
    lane_parts = width // LANES
    base_down = hid
    base_enc = 2 * hid
    base_dec = base_enc + 80
    base_dw = base_dec + 80
    base_small = base_dw + 56

    for i in range(KSIZE * KSIZE):
        taps[i] = jnp.broadcast_to(dw_ref[i : i + 1, :], (8, width))
    dk[...] = jnp.zeros_like(dk)
    up_acc[...] = jnp.zeros_like(up_acc)
    down_acc[...] = jnp.zeros_like(down_acc)
    gres_all[...] = jnp.zeros_like(gres_all)
    pack_ref[base_enc:, :] = jnp.zeros((pack_ref.shape[0] - base_enc, width), F32)
    inside = lax.broadcasted_iota(jnp.int32, (LANES, width), 0) < groups * 8

    @pl.loop(0, wide)
    def _(r):
        enc = dot(x_ref[r], w_enc_ref[...], (0, 0)).astype(BF16).astype(F32)
        for b in range(KSIZE):
            moved = enc if b == 0 else pltpu.roll(enc, LANES - b, 0)
            shifted[b, r] = jnp.where(inside, moved, 0.0)

    conv[:, groups * 8 :, :] = jnp.zeros((rows, LANES - groups * 8, width), F32)

    @pl.loop(0, groups * lane_parts)
    def _(step):
        at = (
            pl.ds(pl.multiple_of((step // lane_parts) * 8, 8), 8),
            pl.ds(pl.multiple_of((step % lane_parts) * LANES, LANES), LANES),
        )
        acc = [None] * rows
        for b in range(KSIZE):
            line = [shifted[(b, r) + at] for r in range(wide)]
            for a in range(KSIZE):
                tap = taps[a * KSIZE + b, :, at[1]]
                for y in range(rows):
                    term = line[y + a] * tap
                    acc[y] = term if acc[y] is None else acc[y] + term
        for y in range(rows):
            conv[(y,) + at] = acc[y]

    gain = gain_ref[...]
    mask = jnp.concatenate([mask_ref[...]] * 2, axis=1)
    gscale = jnp.concatenate([gscale_ref[...]] * 2, axis=1)

    @pl.loop(0, rows // 2)
    def _(step):
        y = step * 2
        cv = conv[pl.ds(y, 2)].reshape(2 * LANES, width)
        centred = cv - jnp.mean(cv, axis=-1, keepdims=True)
        inv_std = lax.rsqrt(jnp.mean(centred * centred, axis=-1, keepdims=True) + 1e-06)
        normed = centred * inv_std
        scaled = (normed * gain).astype(BF16)
        pre = dot(scaled, w_up_ref[...], (1, 0))
        square = pre * pre
        th = jnp.tanh(GELU_C * (pre + GELU_A * (square * pre)))
        half = 0.5 * (1.0 + th)
        act = (pre * half).astype(BF16)
        slope = half + (0.5 * GELU_C) * pre * (1.0 - th * th) * (1.0 + (3.0 * GELU_A) * square)
        centre = shifted[RIM, pl.ds(y + RIM, 2)].reshape(2 * LANES, width)
        residual = (centre + dot(act, w_down_ref[...], (1, 0))).astype(BF16)
        readout = dot(w_dec_t_ref[...], residual, (1, 1))
        base = jnp.concatenate(
            [
                pltpu.roll(x_ref[y + RIM + i].astype(F32), LANES - RIM, 1)
                for i in range(2)
            ],
            axis=1,
        )
        goal = jnp.concatenate([goal_ref[y + i] for i in range(2)], axis=1).astype(F32)
        pred = base + readout
        keep = jnp.where(mask > 0.0, pred, base).astype(BF16)
        pred_ref[y] = keep[:, :LANES]
        pred_ref[y + 1] = keep[:, LANES:]
        misfit = (pred - goal) * mask
        pack_ref[base_small : base_small + 1, :] += jnp.sum(misfit * misfit, axis=0, keepdims=True)
        gout = (misfit * gscale).astype(BF16)
        pack_ref[base_dec : base_dec + chan, :] += dot(gout, residual, (1, 0))
        gres = dot(gout, w_dec_t_ref[...], (0, 0)).astype(BF16)
        gres_all[pl.ds(y + RIM, 2)] = gres.astype(F32).reshape(2, LANES, width)
        down_acc[...] += dot(gres, act, (0, 0))
        gpre = (dot(gres, w_down_ref[...], (1, 1)) * slope).astype(BF16)
        up_acc[...] += dot(scaled, gpre, (0, 0))
        gscaled = dot(gpre, w_up_ref[...], (1, 1))
        pack_ref[base_small + 1 : base_small + 2, :] += jnp.sum(
            gscaled * normed, axis=0, keepdims=True
        )
        g = gscaled * gain
        gconv = inv_std * (
            g
            - jnp.mean(g, axis=-1, keepdims=True)
            - normed * jnp.mean(g * normed, axis=-1, keepdims=True)
        )
        conv[pl.ds(y, 2)] = gconv.reshape(2, LANES, width)

    @pl.loop(0, groups * lane_parts)
    def _(step):
        at = (
            pl.ds(pl.multiple_of((step // lane_parts) * 8, 8), 8),
            pl.ds(pl.multiple_of((step % lane_parts) * LANES, LANES), LANES),
        )
        gc = [conv[(y,) + at] for y in range(rows)]
        for b in range(KSIZE):
            line = [shifted[(b, r) + at] for r in range(wide)]
            for a in range(KSIZE):
                total = gc[0] * line[a]
                for y in range(1, rows):
                    total = total + gc[y] * line[y + a]
                dk[a * KSIZE + b, :, at[1]] += total
            spread = [None] * wide
            for a in range(KSIZE):
                tap = taps[a * KSIZE + b, :, at[1]]
                for y in range(rows):
                    term = gc[y] * tap
                    old = spread[y + a]
                    spread[y + a] = term if old is None else old + term
            for r in range(wide):
                shifted[(b, r) + at] = spread[r]

    @pl.loop(0, wide)
    def _(r):
        g = pltpu.roll(gres_all[r], RIM, 0) + shifted[0, r]
        for b in range(1, KSIZE):
            g = g + pltpu.roll(shifted[b, r], b, 0)
        pack_ref[base_enc : base_enc + chan, :] += dot(x_ref[r], g.astype(BF16), (1, 0))

    for i in range(KSIZE * KSIZE):
        pack_ref[base_dw + i : base_dw + i + 1, :] = jnp.sum(dk[i], axis=0, keepdims=True)
    for k in range(hid // width):
        cols = slice(k * width, (k + 1) * width)
        pack_ref[cols, :] = up_acc[:, cols]
        pack_ref[base_down + k * width : base_down + (k + 1) * width, :] = down_acc[:, cols].T


def shards(state, target, tile_plan, w_enc, dw_kernel, norm_gain, w_up, w_down, w_dec):
    chan, rows, cols = state.shape
    width, hid = w_up.shape
    wide = rows + KSIZE - 1
    tile_cols = cols // PW
    band_at = lax.axis_index("band")
    sub_at = lax.axis_index("sub")
    before, after = with_halo(state, "sub", 2, RIM, True)
    fill = jnp.zeros((chan, rows, LANES - cols - 2 * RIM), BF16)
    lon = jnp.concatenate([before, state, after, fill], axis=2)
    above, below = with_halo(lon, "band", 1, RIM, False)
    x = jnp.concatenate([above, lon, below], axis=1).transpose(1, 0, 2)
    goal = jnp.pad(target.transpose(1, 0, 2), ((0, 0), (0, 0), (0, LANES - cols)))
    plan = lax.dynamic_slice(tile_plan, (band_at, sub_at * tile_cols), (1, tile_cols))
    wet = (plan >= 0).astype(F32)
    mask = jnp.pad(jnp.repeat(wet, PW, axis=1), ((0, 0), (0, LANES - cols)))
    inv_count = 1.0 / (jnp.sum((tile_plan >= 0).astype(F32)) * (chan * PW * PW))
    pack_rows = 2 * hid + 80 + 80 + 56 + 8
    vmem = pl.BlockSpec(memory_space=pltpu.VMEM)
    pred, pack = pl.pallas_call(
        block_kernel,
        out_shape=(
            jax.ShapeDtypeStruct((rows, chan, LANES), BF16),
            jax.ShapeDtypeStruct((pack_rows, width), F32),
        ),
        in_specs=[vmem] * 10,
        out_specs=(vmem, vmem),
        scratch_shapes=[
            pltpu.VMEM((KSIZE, wide, LANES, width), F32),
            pltpu.VMEM((rows, LANES, width), F32),
            pltpu.VMEM((wide, LANES, width), F32),
            pltpu.VMEM((KSIZE * KSIZE, 8, width), F32),
            pltpu.VMEM((KSIZE * KSIZE, 8, width), F32),
            pltpu.VMEM((width, hid), F32),
            pltpu.VMEM((width, hid), F32),
        ],
        compiler_params=pltpu.CompilerParams(vmem_limit_bytes=52 * 1024 * 1024),
        name="block",
    )(
        x, goal, mask, mask * (2.0 * inv_count), w_enc, dw_kernel.astype(F32),
        norm_gain.reshape(1, width), w_up, w_down, w_dec.T,
    )
    new_field = pred[:, :, :cols].transpose(1, 0, 2)
    total = lax.psum(pack, ("band", "sub"))
    g_up = jnp.concatenate([total[k * width : (k + 1) * width] for k in range(hid // width)], axis=1)
    at = 2 * hid
    return (
        new_field,
        (jnp.sum(total[at + 216]) * inv_count).reshape(1),
        total[at : at + chan],
        total[at + 160 : at + 160 + KSIZE * KSIZE],
        total[at + 217],
        g_up,
        total[hid : 2 * hid],
        total[at + 80 : at + 80 + chan].T,
    )


def solution(mesh):
    split = P("groups", "band", "sub")
    parts = P("groups", None)
    return jax.shard_map(
        shards,
        mesh=mesh,
        in_specs=(split, split, parts) + (P(),) * 6,
        out_specs=(split, P("groups"), parts, parts, P("groups"), parts, parts, parts),
        check_vma=False,
    )
```

```python
import functools
import math

import jax
import jax.numpy as jnp
from jax import lax
from jax.experimental import pallas as pl
from jax.experimental.pallas import tpu as pltpu
from jax.sharding import PartitionSpec as P

KSIZE = 7
RIM = 3
PW = 12
LANES = 128
F32 = jnp.float32
BF16 = jnp.bfloat16
GELU_C = math.sqrt(2.0 / math.pi)
GELU_A = 0.044715


def with_halo(value, axis, dim, width, wrap):
    size, length = (lax.axis_size(axis), value.shape[dim])
    up = [(i, (i + 1) % size) for i in range(size if wrap else size - 1)]
    down = [(j, i) for i, j in up]
    last = lax.slice_in_dim(value, length - width, length, axis=dim)
    leading = lax.slice_in_dim(value, 0, width, axis=dim)
    return lax.ppermute(last, axis, up), lax.ppermute(leading, axis, down)


def dot(left, right, dims):
    return lax.dot_general(left, right, ((dims[:1], dims[1:]), ((), ())), preferred_element_type=F32)


def block_kernel(
    x_ref, goal_ref, mask_ref, gscale_ref, w_enc_ref, dw_ref, gain_ref, w_up_ref, w_down_ref,
    w_dec_t_ref, pred_ref, pack_ref, small_ref, shifted, conv, gres_all, taps, dk, up_acc, down_acc,
):
    chan = x_ref.shape[1]
    width = w_enc_ref.shape[1]
    hid = w_up_ref.shape[1]
    rows = goal_ref.shape[0]
    wide = rows + KSIZE - 1
    groups = (LANES - 8) // 8
    lane_parts = width // LANES
    base_down = hid
    base_enc = 2 * hid
    base_dec = base_enc + 80
    base_dw = base_dec + 80

    for i in range(KSIZE * KSIZE):
        taps[i] = jnp.broadcast_to(dw_ref[i : i + 1, :], (8, width))
    dk[...] = jnp.zeros_like(dk)
    up_acc[...] = jnp.zeros_like(up_acc)
    down_acc[...] = jnp.zeros_like(down_acc)
    gres_all[...] = jnp.zeros_like(gres_all)
    pack_ref[base_enc:, :] = jnp.zeros((pack_ref.shape[0] - base_enc, width), F32)
    small_ref[...] = jnp.zeros_like(small_ref)
    inside = lax.broadcasted_iota(jnp.int32, (LANES, width), 0) < groups * 8

    @pl.loop(0, wide)
    def _(r):
        enc = dot(x_ref[r], w_enc_ref[...], (0, 0)).astype(BF16).astype(F32)
        for b in range(KSIZE):
            moved = enc if b == 0 else pltpu.roll(enc, LANES - b, 0)
            shifted[b, r] = jnp.where(inside, moved, 0.0)

    conv[:, groups * 8 :, :] = jnp.zeros((rows, LANES - groups * 8, width), F32)

    @pl.loop(0, groups * lane_parts)
    def _(step):
        at = (
            pl.ds(pl.multiple_of((step // lane_parts) * 8, 8), 8),
            pl.ds(pl.multiple_of((step % lane_parts) * LANES, LANES), LANES),
        )
        acc = [None] * rows
        for b in range(KSIZE):
            line = [shifted[(b, r) + at] for r in range(wide)]
            for a in range(KSIZE):
                tap = taps[a * KSIZE + b, :, at[1]]
                for y in range(rows):
                    term = line[y + a] * tap
                    acc[y] = term if acc[y] is None else acc[y] + term
        for y in range(rows):
            conv[(y,) + at] = acc[y]

    gain = gain_ref[...]
    mask = jnp.concatenate([mask_ref[...]] * 2, axis=1)
    gscale = jnp.concatenate([gscale_ref[...]] * 2, axis=1)

    @pl.loop(0, rows // 2)
    def _(step):
        y = step * 2
        cv = conv[pl.ds(y, 2)].reshape(2 * LANES, width)
        centred = cv - jnp.mean(cv, axis=-1, keepdims=True)
        inv_std = lax.rsqrt(jnp.mean(centred * centred, axis=-1, keepdims=True) + 1e-06)
        normed = centred * inv_std
        scaled = (normed * gain).astype(BF16)
        pre = dot(scaled, w_up_ref[...], (1, 0))
        square = pre * pre
        th = jnp.tanh(GELU_C * (pre + GELU_A * (square * pre)))
        half = 0.5 * (1.0 + th)
        act = (pre * half).astype(BF16)
        slope = half + (0.5 * GELU_C) * pre * (1.0 - th * th) * (1.0 + (3.0 * GELU_A) * square)
        centre = shifted[RIM, pl.ds(y + RIM, 2)].reshape(2 * LANES, width)
        residual = (centre + dot(act, w_down_ref[...], (1, 0))).astype(BF16)
        readout = dot(w_dec_t_ref[...], residual, (1, 1))
        base = jnp.concatenate(
            [
                pltpu.roll(x_ref[y + RIM + i].astype(F32), LANES - RIM, 1)
                for i in range(2)
            ],
            axis=1,
        )
        goal = jnp.concatenate([goal_ref[y + i] for i in range(2)], axis=1).astype(F32)
        pred = base + readout
        keep = jnp.where(mask > 0.0, pred, base).astype(BF16)
        pred_ref[y] = keep[:, :LANES]
        pred_ref[y + 1] = keep[:, LANES:]
        misfit = (pred - goal) * mask
        small_ref[0:1, :] += jnp.sum(misfit * misfit, axis=0, keepdims=True)
        gout = (misfit * gscale).astype(BF16)
        pack_ref[base_dec : base_dec + chan, :] += dot(gout, residual, (1, 0))
        gres = dot(gout, w_dec_t_ref[...], (0, 0)).astype(BF16)
        gres_all[pl.ds(y + RIM, 2)] = gres.astype(F32).reshape(2, LANES, width)
        down_acc[...] += dot(gres, act, (0, 0))
        gpre = (dot(gres, w_down_ref[...], (1, 1)) * slope).astype(BF16)
        up_acc[...] += dot(scaled, gpre, (0, 0))
        gscaled = dot(gpre, w_up_ref[...], (1, 1))
        small_ref[1:2, :] += jnp.sum(
            gscaled * normed, axis=0, keepdims=True
        )
        g = gscaled * gain
        gconv = inv_std * (
            g
            - jnp.mean(g, axis=-1, keepdims=True)
            - normed * jnp.mean(g * normed, axis=-1, keepdims=True)
        )
        conv[pl.ds(y, 2)] = gconv.reshape(2, LANES, width)

    @pl.loop(0, groups * lane_parts)
    def _(step):
        at = (
            pl.ds(pl.multiple_of((step // lane_parts) * 8, 8), 8),
            pl.ds(pl.multiple_of((step % lane_parts) * LANES, LANES), LANES),
        )
        gc = [conv[(y,) + at] for y in range(rows)]
        for b in range(KSIZE):
            line = [shifted[(b, r) + at] for r in range(wide)]
            for a in range(KSIZE):
                total = gc[0] * line[a]
                for y in range(1, rows):
                    total = total + gc[y] * line[y + a]
                dk[a * KSIZE + b, :, at[1]] += total
            spread = [None] * wide
            for a in range(KSIZE):
                tap = taps[a * KSIZE + b, :, at[1]]
                for y in range(rows):
                    term = gc[y] * tap
                    old = spread[y + a]
                    spread[y + a] = term if old is None else old + term
            for r in range(wide):
                shifted[(b, r) + at] = spread[r]

    @pl.loop(0, wide)
    def _(r):
        g = pltpu.roll(gres_all[r], RIM, 0) + shifted[0, r]
        for b in range(1, KSIZE):
            g = g + pltpu.roll(shifted[b, r], b, 0)
        pack_ref[base_enc : base_enc + chan, :] += dot(x_ref[r], g.astype(BF16), (1, 0))

    for i in range(KSIZE * KSIZE):
        pack_ref[base_dw + i : base_dw + i + 1, :] = jnp.sum(dk[i], axis=0, keepdims=True)
    for k in range(hid // width):
        cols = slice(k * width, (k + 1) * width)
        pack_ref[cols, :] = up_acc[:, cols]
        pack_ref[base_down + k * width : base_down + (k + 1) * width, :] = down_acc[:, cols].T


def sum_kernel(
    ranges, band_size, pack_ref, small_ref, up_ref, down_ref, enc_ref, dw_ref, dec_ref, small_out,
    acc, core_in, out_buf, in_buf, res, small_now, small_in, send_sem, recv_sem, small_send, small_recv,
):
    band = lax.axis_index("band")
    sub = lax.axis_index("sub")
    bits = band_size.bit_length() - 1
    core = {"band": band, "sub": 1 - sub}

    def digit(bit):
        return (band // (1 << bit)) % 2

    def across(bit):
        return {"band": band + (1 - 2 * digit(bit)) * (1 << bit), "sub": sub}

    barrier = pltpu.get_barrier_semaphore()
    for peer in [core] + [across(bit) for bit in range(bits)]:
        pl.semaphore_signal(barrier, inc=1, device_id=peer, device_id_type=pl.DeviceIdType.MESH)
    pl.semaphore_wait(barrier, bits + 1)

    started = []

    def send(src, dst, send_at, recv_at, peer):
        copy = pltpu.make_async_remote_copy(
            src_ref=src, dst_ref=dst, send_sem=send_at, recv_sem=recv_at,
            device_id=peer, device_id_type=pl.DeviceIdType.MESH,
        )
        copy.start()
        started.append(copy)
        return copy

    def rows_at(start, size):
        return pl.ds(pl.multiple_of(start, 16), size)

    small_now[0] = small_ref[...]

    def send_small(step, peer):
        return send(
            small_now.at[step], small_in.at[step], small_send.at[step], small_recv.at[step], peer
        )

    def add_small(step, copy):
        copy.wait_recv()
        small_now[step + 1] = small_now[step] + small_in[step]

    small_copy = send_small(0, core)
    first = []
    place = 0
    for h, (base, size) in enumerate(ranges):
        half = size // 2
        first.append(
            (
                place,
                send(
                    pack_ref.at[rows_at(base + (1 - sub) * half, half)],
                    core_in.at[pl.ds(place, half)],
                    send_sem.at[h, 0], recv_sem.at[h, 0], core,
                ),
            )
        )
        place += half
    add_small(0, small_copy)
    offset = []
    for h, (base, size) in enumerate(ranges):
        half = size // 2
        place, copy = first[h]
        at = base + sub * half
        copy.wait_recv()
        acc[rows_at(at, half), :] = pack_ref[rows_at(at, half), :] + core_in[place : place + half, :]
        offset.append(at)

    length = [size // 2 for _, size in ranges]
    slot = 0
    for step in range(bits):
        flying = []
        small_copy = send_small(step + 1, across(step))
        for h in range(len(ranges)):
            bit = (step + h) % bits
            half = length[h] // 2
            mine = digit(bit)
            other = offset[h] + (1 - mine) * half
            out_buf[slot : slot + half, :] = acc[rows_at(other, half), :].astype(BF16)
            flying.append(
                (
                    slot,
                    send(
                        out_buf.at[pl.ds(slot, half)], in_buf.at[pl.ds(slot, half)],
                        send_sem.at[h, step + 1], recv_sem.at[h, step + 1], across(bit),
                    ),
                )
            )
            offset[h] = offset[h] + mine * half
            length[h] = half
            slot += half
        add_small(step + 1, small_copy)
        for h in range(len(ranges)):
            place, copy = flying[h]
            copy.wait_recv()
            rows = rows_at(offset[h], length[h])
            value = acc[rows, :] + in_buf[place : place + length[h], :].astype(F32)
            if step < bits - 1:
                acc[rows, :] = value
            else:
                res[rows, :] = value.astype(BF16)

    for step in range(bits + 1):
        flying = []
        for h in range(len(ranges)):
            last = step == bits
            bit = (bits - 1 - step + h) % bits
            mine = sub if last else digit(bit)
            rows = rows_at(offset[h], length[h])
            at = bits + 1 + step
            flying.append(
                send(
                    res.at[rows], res.at[rows], send_sem.at[h, at], recv_sem.at[h, at],
                    core if last else across(bit),
                )
            )
            offset[h] = offset[h] - mine * length[h]
            length[h] = 2 * length[h]
        for copy in flying:
            copy.wait_recv()

    small_out[...] = small_now[bits + 1]
    width = pack_ref.shape[1]
    hid = down_ref.shape[0]
    chan = enc_ref.shape[0]
    for k in range(hid // width):
        up_ref[:, k * width : (k + 1) * width] = res[k * width : (k + 1) * width, :]
    down_ref[...] = res[hid : 2 * hid, :]
    at = 2 * hid
    enc_ref[...] = res[at : at + 80, :][:chan]
    dec_ref[...] = res[at + 80 : at + 160, :][:chan]
    dw_ref[...] = res[at + 160 : at + 224, :][: dw_ref.shape[0]]
    for copy in started:
        copy.wait_send()


def summed(pack, small, chan, hid):
    total, width = pack.shape
    band_size = lax.axis_size("band")
    bits = band_size.bit_length() - 1
    unit = 32 * band_size
    front = -(-(total // unit) // 2) * unit
    ranges = [(0, front)] if total == front else [(0, front), (front, total - front)]
    parts = len(ranges)
    staged = sum(size // 2 // (1 << (s + 1)) for _, size in ranges for s in range(bits))
    vmem = pl.BlockSpec(memory_space=pltpu.VMEM)
    dma = pltpu.SemaphoreType.DMA
    up, down, enc, dw, dec, small = pl.pallas_call(
        functools.partial(sum_kernel, ranges, band_size),
        out_shape=(
            jax.ShapeDtypeStruct((width, hid), BF16),
            jax.ShapeDtypeStruct((hid, width), BF16),
            jax.ShapeDtypeStruct((chan, width), BF16),
            jax.ShapeDtypeStruct((KSIZE * KSIZE, width), BF16),
            jax.ShapeDtypeStruct((chan, width), BF16),
            jax.ShapeDtypeStruct((8, width), F32),
        ),
        in_specs=[vmem] * 2,
        out_specs=(vmem,) * 6,
        scratch_shapes=[
            pltpu.VMEM((total, width), F32),
            pltpu.VMEM((total // 2, width), F32),
            pltpu.VMEM((staged, width), BF16),
            pltpu.VMEM((staged, width), BF16),
            pltpu.VMEM((total, width), BF16),
            pltpu.VMEM((bits + 2, 8, width), F32),
            pltpu.VMEM((bits + 1, 8, width), F32),
            dma((parts, 2 * bits + 2)),
            dma((parts, 2 * bits + 2)),
            dma((bits + 1,)),
            dma((bits + 1,)),
        ],
        compiler_params=pltpu.CompilerParams(
            collective_id=0, has_side_effects=True, vmem_limit_bytes=40 * 1024 * 1024
        ),
        name="grad_sum",
    )(pack, small)
    return up, down, enc, dw, dec.T, small


def shards(state, target, tile_plan, w_enc, dw_kernel, norm_gain, w_up, w_down, w_dec):
    chan, rows, cols = state.shape
    width, hid = w_up.shape
    wide = rows + KSIZE - 1
    tile_cols = cols // PW
    band_at = lax.axis_index("band")
    sub_at = lax.axis_index("sub")
    before, after = with_halo(state, "sub", 2, RIM, True)
    fill = jnp.zeros((chan, rows, LANES - cols - 2 * RIM), BF16)
    lon = jnp.concatenate([before, state, after, fill], axis=2)
    above, below = with_halo(lon, "band", 1, RIM, False)
    x = jnp.concatenate([above, lon, below], axis=1).transpose(1, 0, 2)
    goal = jnp.pad(target.transpose(1, 0, 2), ((0, 0), (0, 0), (0, LANES - cols)))
    plan = lax.dynamic_slice(tile_plan, (band_at, sub_at * tile_cols), (1, tile_cols))
    wet = (plan >= 0).astype(F32)
    mask = jnp.pad(jnp.repeat(wet, PW, axis=1), ((0, 0), (0, LANES - cols)))
    inv_count = 1.0 / (jnp.sum((tile_plan >= 0).astype(F32)) * (chan * PW * PW))
    members = lax.axis_size("band") * lax.axis_size("sub")
    pack_rows = -(-(2 * hid + 80 + 80 + 64) // (16 * members)) * 16 * members
    vmem = pl.BlockSpec(memory_space=pltpu.VMEM)
    pred, pack, small = pl.pallas_call(
        block_kernel,
        out_shape=(
            jax.ShapeDtypeStruct((rows, chan, LANES), BF16),
            jax.ShapeDtypeStruct((pack_rows, width), F32),
            jax.ShapeDtypeStruct((8, width), F32),
        ),
        in_specs=[vmem] * 10,
        out_specs=(vmem,) * 3,
        scratch_shapes=[
            pltpu.VMEM((KSIZE, wide, LANES, width), F32),
            pltpu.VMEM((rows, LANES, width), F32),
            pltpu.VMEM((wide, LANES, width), F32),
            pltpu.VMEM((KSIZE * KSIZE, 8, width), F32),
            pltpu.VMEM((KSIZE * KSIZE, 8, width), F32),
            pltpu.VMEM((width, hid), F32),
            pltpu.VMEM((width, hid), F32),
        ],
        compiler_params=pltpu.CompilerParams(vmem_limit_bytes=52 * 1024 * 1024),
        name="block",
    )(
        x, goal, mask, mask * (2.0 * inv_count), w_enc, dw_kernel.astype(F32),
        norm_gain.reshape(1, width), w_up, w_down, w_dec.T,
    )
    new_field = pred[:, :, :cols].transpose(1, 0, 2)
    g_up, g_down, g_enc, g_dw, g_dec, small = summed(pack, small, chan, hid)
    return (
        new_field,
        (jnp.sum(small[0]) * inv_count).reshape(1),
        g_enc.astype(F32),
        g_dw.astype(F32),
        small[1],
        g_up.astype(F32),
        g_down.astype(F32),
        g_dec.astype(F32),
    )


def solution(mesh):
    split = P("groups", "band", "sub")
    parts = P("groups", None)
    return jax.shard_map(
        shards,
        mesh=mesh,
        in_specs=(split, split, parts) + (P(),) * 6,
        out_specs=(split, P("groups"), parts, parts, P("groups"), parts, parts, parts),
        check_vma=False,
    )
```

```python
import functools
import math

import jax
import jax.numpy as jnp
from jax import lax
from jax.experimental import pallas as pl
from jax.experimental.pallas import tpu as pltpu
from jax.sharding import PartitionSpec as P

KSIZE = 7
RIM = 3
PW = 12
LANES = 128
F32 = jnp.float32
BF16 = jnp.bfloat16
GELU_C = math.sqrt(2.0 / math.pi)
GELU_A = 0.044715


def with_halo(value, axis, dim, width, wrap):
    size, length = (lax.axis_size(axis), value.shape[dim])
    up = [(i, (i + 1) % size) for i in range(size if wrap else size - 1)]
    down = [(j, i) for i, j in up]
    last = lax.slice_in_dim(value, length - width, length, axis=dim)
    leading = lax.slice_in_dim(value, 0, width, axis=dim)
    return lax.ppermute(last, axis, up), lax.ppermute(leading, axis, down)


def dot(left, right, dims):
    return lax.dot_general(left, right, ((dims[:1], dims[1:]), ((), ())), preferred_element_type=F32)


def rows_at(start, size):
    return pl.ds(pl.multiple_of(start, 16), size)


def block_kernel(
    ranges, band_size, x_ref, goal_ref, mask_ref, gscale_ref, w_enc_ref, dw_ref, gain_ref, w_up_ref,
    w_down_ref, w_dec_t_ref, pred_ref, small_out, up_ref, down_ref, enc_ref, dw_out, dec_ref,
    shifted, conv, gres_all, taps, dk, up_acc, down_acc, acc, core_in, out_buf, in_buf, res,
    small_now, small_in, send_sem, recv_sem, small_send, small_recv,
):
    chan = x_ref.shape[1]
    width = w_enc_ref.shape[1]
    hid = w_up_ref.shape[1]
    rows = goal_ref.shape[0]
    wide = rows + KSIZE - 1
    groups = (LANES - 8) // 8
    lane_parts = width // LANES
    base_enc = 2 * hid
    base_dec = base_enc + 80
    base_dw = base_dec + 80

    band = lax.axis_index("band")
    sub = lax.axis_index("sub")
    bits = band_size.bit_length() - 1
    core = {"band": band, "sub": 1 - sub}
    started = []

    def digit(bit):
        return (band // (1 << bit)) % 2

    def across(bit):
        return {"band": band + (1 - 2 * digit(bit)) * (1 << bit), "sub": sub}

    barrier = pltpu.get_barrier_semaphore()
    for peer in [core] + [across(bit) for bit in range(bits)]:
        pl.semaphore_signal(barrier, inc=1, device_id=peer, device_id_type=pl.DeviceIdType.MESH)

    def send(src, dst, send_at, recv_at, peer):
        copy = pltpu.make_async_remote_copy(
            src_ref=src, dst_ref=dst, send_sem=send_at, recv_sem=recv_at,
            device_id=peer, device_id_type=pl.DeviceIdType.MESH,
        )
        copy.start()
        started.append(copy)
        return copy

    def send_small(step, peer):
        return send(
            small_now.at[step], small_in.at[step], small_send.at[step], small_recv.at[step], peer
        )

    def add_small(step, copy):
        copy.wait_recv()
        small_now[step + 1] = small_now[step] + small_in[step]

    def exchange(parts, with_small):
        small_copy = send_small(0, core) if with_small else None
        first = []
        offset = {}
        length = {}
        for h in parts:
            base, size, core_at, _ = ranges[h]
            half = size // 2
            first.append(
                send(
                    acc.at[rows_at(base + (1 - sub) * half, half)],
                    core_in.at[pl.ds(core_at, half)],
                    send_sem.at[h, 0], recv_sem.at[h, 0], core,
                )
            )
            offset[h] = base + sub * half
            length[h] = half
        yield
        if with_small:
            add_small(0, small_copy)
        for h, copy in zip(parts, first):
            copy.wait_recv()
            at = rows_at(offset[h], length[h])
            core_at = ranges[h][2]
            acc[at, :] = acc[at, :] + core_in[core_at : core_at + length[h], :]
        slots = {h: ranges[h][3] for h in parts}
        for step in range(bits):
            flying = []
            if with_small:
                small_copy = send_small(step + 1, across(step))
            for h in parts:
                bit = (step + h) % bits
                half = length[h] // 2
                mine = digit(bit)
                slot = slots[h]
                other = offset[h] + (1 - mine) * half
                out_buf[slot : slot + half, :] = acc[rows_at(other, half), :].astype(BF16)
                flying.append(
                    (
                        slot,
                        send(
                            out_buf.at[pl.ds(slot, half)], in_buf.at[pl.ds(slot, half)],
                            send_sem.at[h, step + 1], recv_sem.at[h, step + 1], across(bit),
                        ),
                    )
                )
                offset[h] = offset[h] + mine * half
                length[h] = half
                slots[h] = slot + half
            yield
            if with_small:
                add_small(step + 1, small_copy)
            for h, (place, copy) in zip(parts, flying):
                copy.wait_recv()
                at = rows_at(offset[h], length[h])
                value = acc[at, :] + in_buf[place : place + length[h], :].astype(F32)
                if step < bits - 1:
                    acc[at, :] = value
                else:
                    res[at, :] = value.astype(BF16)
        for step in range(bits + 1):
            flying = []
            for h in parts:
                last = step == bits
                bit = (bits - 1 - step + h) % bits
                mine = sub if last else digit(bit)
                at = rows_at(offset[h], length[h])
                sem = bits + 1 + step
                flying.append(
                    send(
                        res.at[at], res.at[at], send_sem.at[h, sem], recv_sem.at[h, sem],
                        core if last else across(bit),
                    )
                )
                offset[h] = offset[h] - mine * length[h]
                length[h] = 2 * length[h]
            yield
            for copy in flying:
                copy.wait_recv()

    for i in range(KSIZE * KSIZE):
        taps[i] = jnp.broadcast_to(dw_ref[i : i + 1, :], (8, width))
    dk[...] = jnp.zeros_like(dk)
    up_acc[...] = jnp.zeros_like(up_acc)
    down_acc[...] = jnp.zeros_like(down_acc)
    gres_all[...] = jnp.zeros_like(gres_all)
    acc[base_enc:, :] = jnp.zeros((acc.shape[0] - base_enc, width), F32)
    small_now[0] = jnp.zeros((8, width), F32)
    inside = lax.broadcasted_iota(jnp.int32, (LANES, width), 0) < groups * 8

    @pl.loop(0, wide)
    def _(r):
        enc = dot(x_ref[r], w_enc_ref[...], (0, 0)).astype(BF16).astype(F32)
        for b in range(KSIZE):
            moved = enc if b == 0 else pltpu.roll(enc, LANES - b, 0)
            shifted[b, r] = jnp.where(inside, moved, 0.0)

    conv[:, groups * 8 :, :] = jnp.zeros((rows, LANES - groups * 8, width), F32)

    def part_of(step):
        return (
            pl.ds(pl.multiple_of((step // lane_parts) * 8, 8), 8),
            pl.ds(pl.multiple_of((step % lane_parts) * LANES, LANES), LANES),
        )

    @pl.loop(0, groups * lane_parts)
    def _(step):
        at = part_of(step)
        total = jnp.zeros((rows, 8, LANES), F32)
        for b in range(KSIZE):
            line = shifted[(b, slice(None)) + at]
            for a in range(KSIZE):
                total = total + line[a : a + rows] * taps[a * KSIZE + b, :, at[1]][None]
        conv[(slice(None),) + at] = total

    gain = gain_ref[...]
    mask = jnp.concatenate([mask_ref[...]] * 2, axis=1)
    gscale = jnp.concatenate([gscale_ref[...]] * 2, axis=1)

    @pl.loop(0, rows // 2)
    def _(step):
        y = step * 2
        cv = conv[pl.ds(y, 2)].reshape(2 * LANES, width)
        centred = cv - jnp.mean(cv, axis=-1, keepdims=True)
        inv_std = lax.rsqrt(jnp.mean(centred * centred, axis=-1, keepdims=True) + 1e-06)
        normed = centred * inv_std
        scaled = (normed * gain).astype(BF16)
        pre = dot(scaled, w_up_ref[...], (1, 0))
        square = pre * pre
        th = jnp.tanh(GELU_C * (pre + GELU_A * (square * pre)))
        half = 0.5 * (1.0 + th)
        act = (pre * half).astype(BF16)
        slope = half + (0.5 * GELU_C) * pre * (1.0 - th * th) * (1.0 + (3.0 * GELU_A) * square)
        centre = shifted[RIM, pl.ds(y + RIM, 2)].reshape(2 * LANES, width)
        residual = (centre + dot(act, w_down_ref[...], (1, 0))).astype(BF16)
        readout = dot(w_dec_t_ref[...], residual, (1, 1))
        base = jnp.concatenate(
            [
                pltpu.roll(x_ref[y + RIM + i].astype(F32), LANES - RIM, 1)
                for i in range(2)
            ],
            axis=1,
        )
        goal = jnp.concatenate([goal_ref[y + i] for i in range(2)], axis=1).astype(F32)
        pred = base + readout
        keep = jnp.where(mask > 0.0, pred, base).astype(BF16)
        pred_ref[y] = keep[:, :LANES]
        pred_ref[y + 1] = keep[:, LANES:]
        misfit = (pred - goal) * mask
        small_now[0, 0:1, :] += jnp.sum(misfit * misfit, axis=0, keepdims=True)
        gout = (misfit * gscale).astype(BF16)
        acc[base_dec : base_dec + chan, :] += dot(gout, residual, (1, 0))
        gres = dot(gout, w_dec_t_ref[...], (0, 0)).astype(BF16)
        gres_all[pl.ds(y + RIM, 2)] = gres.astype(F32).reshape(2, LANES, width)
        down_acc[...] += dot(gres, act, (0, 0))
        gpre = (dot(gres, w_down_ref[...], (1, 1)) * slope).astype(BF16)
        up_acc[...] += dot(scaled, gpre, (0, 0))
        gscaled = dot(gpre, w_up_ref[...], (1, 1))
        small_now[0, 1:2, :] += jnp.sum(gscaled * normed, axis=0, keepdims=True)
        g = gscaled * gain
        gconv = inv_std * (
            g
            - jnp.mean(g, axis=-1, keepdims=True)
            - normed * jnp.mean(g * normed, axis=-1, keepdims=True)
        )
        conv[pl.ds(y, 2)] = gconv.reshape(2, LANES, width)

    for k in range(hid // width):
        cols = slice(k * width, (k + 1) * width)
        acc[cols, :] = up_acc[:, cols]
        acc[hid + k * width : hid + (k + 1) * width, :] = down_acc[:, cols].T

    pl.semaphore_wait(barrier, bits + 1)
    flow = exchange([0, 1], True)
    next(flow)

    def depthwise_back(step):
        at = part_of(step)
        gc = conv[(slice(None),) + at]
        gc_rows = [gc[y] for y in range(rows)]
        for b in range(KSIZE):
            line = shifted[(b, slice(None)) + at]
            for a in range(KSIZE):
                dk[a * KSIZE + b, :, at[1]] += jnp.sum(gc * line[a : a + rows], axis=0)
            spread = [None] * wide
            for a in range(KSIZE):
                tap = taps[a * KSIZE + b, :, at[1]]
                for y in range(rows):
                    term = gc_rows[y] * tap
                    old = spread[y + a]
                    spread[y + a] = term if old is None else old + term
            for r in range(wide):
                shifted[(b, r) + at] = spread[r]

    def encoder_back(r):
        g = pltpu.roll(gres_all[r], RIM, 0) + shifted[0, r]
        for b in range(1, KSIZE):
            g = g + pltpu.roll(shifted[b, r], b, 0)
        acc[base_enc : base_enc + chan, :] += dot(x_ref[r], g.astype(BF16), (1, 0))

    steps = groups * lane_parts
    for piece in range(6):
        pl.loop(piece * steps // 6, (piece + 1) * steps // 6)(depthwise_back)
        next(flow, None)
    for piece in range(2):
        pl.loop(piece * wide // 2, (piece + 1) * wide // 2)(encoder_back)
        next(flow, None)
    for i in range(KSIZE * KSIZE):
        acc[base_dw + i : base_dw + i + 1, :] = jnp.sum(dk[i], axis=0, keepdims=True)
    for _ in flow:
        pass

    tail = exchange([2], False)
    next(tail)
    small_out[...] = small_now[bits + 1]
    for k in range(hid // width):
        up_ref[:, k * width : (k + 1) * width] = res[k * width : (k + 1) * width, :]
    down_ref[...] = res[hid : 2 * hid, :]
    for _ in tail:
        pass
    enc_ref[...] = res[base_enc : base_enc + 80, :][:chan]
    dec_ref[...] = res[base_dec : base_dec + 80, :][:chan]
    dw_out[...] = res[base_dw : base_dw + 64, :][: dw_out.shape[0]]
    for copy in started:
        copy.wait_send()


def shards(state, target, tile_plan, w_enc, dw_kernel, norm_gain, w_up, w_down, w_dec):
    chan, rows, cols = state.shape
    width, hid = w_up.shape
    wide = rows + KSIZE - 1
    tile_cols = cols // PW
    band_at = lax.axis_index("band")
    sub_at = lax.axis_index("sub")
    before, after = with_halo(state, "sub", 2, RIM, True)
    fill = jnp.zeros((chan, rows, LANES - cols - 2 * RIM), BF16)
    lon = jnp.concatenate([before, state, after, fill], axis=2)
    above, below = with_halo(lon, "band", 1, RIM, False)
    x = jnp.concatenate([above, lon, below], axis=1).transpose(1, 0, 2)
    goal = jnp.pad(target.transpose(1, 0, 2), ((0, 0), (0, 0), (0, LANES - cols)))
    plan = lax.dynamic_slice(tile_plan, (band_at, sub_at * tile_cols), (1, tile_cols))
    wet = (plan >= 0).astype(F32)
    mask = jnp.pad(jnp.repeat(wet, PW, axis=1), ((0, 0), (0, LANES - cols)))
    inv_count = 1.0 / (jnp.sum((tile_plan >= 0).astype(F32)) * (chan * PW * PW))
    band_size = lax.axis_size("band")
    bits = band_size.bit_length() - 1
    unit = 32 * band_size
    cuts = [hid, hid, -(-(80 + 80 + 64) // unit) * unit]
    ranges = []
    base = staged = 0
    for size in cuts:
        ranges.append((base, size, base // 2, staged))
        base += size
        staged += sum(size // 2 // (1 << (s + 1)) for s in range(bits))
    vmem = pl.BlockSpec(memory_space=pltpu.VMEM)
    dma = pltpu.SemaphoreType.DMA
    pred, small, g_up, g_down, g_enc, g_dw, g_dec = pl.pallas_call(
        functools.partial(block_kernel, ranges, band_size),
        out_shape=(
            jax.ShapeDtypeStruct((rows, chan, LANES), BF16),
            jax.ShapeDtypeStruct((8, width), F32),
            jax.ShapeDtypeStruct((width, hid), BF16),
            jax.ShapeDtypeStruct((hid, width), BF16),
            jax.ShapeDtypeStruct((chan, width), BF16),
            jax.ShapeDtypeStruct((KSIZE * KSIZE, width), BF16),
            jax.ShapeDtypeStruct((chan, width), BF16),
        ),
        in_specs=[vmem] * 10,
        out_specs=(vmem,) * 7,
        scratch_shapes=[
            pltpu.VMEM((KSIZE, wide, LANES, width), F32),
            pltpu.VMEM((rows, LANES, width), F32),
            pltpu.VMEM((wide, LANES, width), F32),
            pltpu.VMEM((KSIZE * KSIZE, 8, width), F32),
            pltpu.VMEM((KSIZE * KSIZE, 8, width), F32),
            pltpu.VMEM((width, hid), F32),
            pltpu.VMEM((width, hid), F32),
            pltpu.VMEM((base, width), F32),
            pltpu.VMEM((base // 2, width), F32),
            pltpu.VMEM((staged, width), BF16),
            pltpu.VMEM((staged, width), BF16),
            pltpu.VMEM((base, width), BF16),
            pltpu.VMEM((bits + 2, 8, width), F32),
            pltpu.VMEM((bits + 1, 8, width), F32),
            dma((3, 2 * bits + 2)),
            dma((3, 2 * bits + 2)),
            dma((bits + 1,)),
            dma((bits + 1,)),
        ],
        compiler_params=pltpu.CompilerParams(
            collective_id=0, has_side_effects=True, vmem_limit_bytes=52 * 1024 * 1024
        ),
        name="block",
    )(
        x, goal, mask, mask * (2.0 * inv_count), w_enc, dw_kernel.astype(F32),
        norm_gain.reshape(1, width), w_up, w_down, w_dec.T,
    )
    new_field = pred[:, :, :cols].transpose(1, 0, 2)
    return (
        new_field,
        (jnp.sum(small[0]) * inv_count).reshape(1),
        g_enc.astype(F32),
        g_dw.astype(F32),
        small[1],
        g_up.astype(F32),
        g_down.astype(F32),
        g_dec.T.astype(F32),
    )


def solution(mesh):
    split = P("groups", "band", "sub")
    parts = P("groups", None)
    return jax.shard_map(
        shards,
        mesh=mesh,
        in_specs=(split, split, parts) + (P(),) * 6,
        out_specs=(split, P("groups"), parts, parts, P("groups"), parts, parts, parts),
        check_vma=False,
    )
```

```python
import functools
import math

import jax
import jax.numpy as jnp
from jax import lax
from jax.experimental import pallas as pl
from jax.experimental.pallas import tpu as pltpu
from jax.sharding import PartitionSpec as P

KSIZE = 7
RIM = 3
PW = 12
LANES = 128
F32 = jnp.float32
BF16 = jnp.bfloat16
GELU_C = math.sqrt(2.0 / math.pi)
GELU_A = 0.044715


def with_halo(value, axis, dim, width, wrap):
    size, length = (lax.axis_size(axis), value.shape[dim])
    up = [(i, (i + 1) % size) for i in range(size if wrap else size - 1)]
    down = [(j, i) for i, j in up]
    last = lax.slice_in_dim(value, length - width, length, axis=dim)
    leading = lax.slice_in_dim(value, 0, width, axis=dim)
    return lax.ppermute(last, axis, up), lax.ppermute(leading, axis, down)


def dot(left, right, dims):
    return lax.dot_general(left, right, ((dims[:1], dims[1:]), ((), ())), preferred_element_type=F32)


def rows_at(start, size):
    return pl.ds(pl.multiple_of(start, 16), size)


def block_kernel(
    ranges, band_size, x_ref, goal_ref, mask_ref, gscale_ref, w_enc_ref, dw_ref, gain_ref, w_up_ref,
    w_down_ref, w_dec_t_ref, pred_ref, small_out, up_ref, down_ref, enc_ref, dw_out, dec_ref,
    shifted, conv, gres_all, taps, dk, up_acc, down_acc, acc, core_in, out_buf, in_buf, res,
    small_now, small_in, send_sem, recv_sem, small_send, small_recv,
):
    chan = x_ref.shape[1]
    width = w_enc_ref.shape[1]
    hid = w_up_ref.shape[1]
    rows = goal_ref.shape[0]
    wide = rows + KSIZE - 1
    groups = (LANES - 8) // 8
    lane_parts = width // LANES
    base_enc = 2 * hid
    base_dec = base_enc + 80
    base_dw = base_dec + 80

    band = lax.axis_index("band")
    sub = lax.axis_index("sub")
    bits = band_size.bit_length() - 1
    core = {"band": band, "sub": 1 - sub}
    started = []

    def digit(bit):
        return (band // (1 << bit)) % 2

    def across(bit):
        return {"band": band + (1 - 2 * digit(bit)) * (1 << bit), "sub": sub}

    barrier = pltpu.get_barrier_semaphore()
    for peer in [core] + [across(bit) for bit in range(bits)]:
        pl.semaphore_signal(barrier, inc=1, device_id=peer, device_id_type=pl.DeviceIdType.MESH)

    def send(src, dst, send_at, recv_at, peer):
        copy = pltpu.make_async_remote_copy(
            src_ref=src, dst_ref=dst, send_sem=send_at, recv_sem=recv_at,
            device_id=peer, device_id_type=pl.DeviceIdType.MESH,
        )
        copy.start()
        started.append(copy)
        return copy

    def send_small(step, peer):
        return send(
            small_now.at[step], small_in.at[step], small_send.at[step], small_recv.at[step], peer
        )

    def add_small(step, copy):
        copy.wait_recv()
        small_now[step + 1] = small_now[step] + small_in[step]

    def exchange(parts, with_small):
        small_copy = send_small(0, core) if with_small else None
        first = []
        offset = {}
        length = {}
        for h in parts:
            base, size, core_at, _ = ranges[h]
            half = size // 2
            first.append(
                send(
                    acc.at[rows_at(base + (1 - sub) * half, half)],
                    core_in.at[pl.ds(core_at, half)],
                    send_sem.at[h, 0], recv_sem.at[h, 0], core,
                )
            )
            offset[h] = base + sub * half
            length[h] = half
        yield
        if with_small:
            add_small(0, small_copy)
        for h, copy in zip(parts, first):
            copy.wait_recv()
            at = rows_at(offset[h], length[h])
            core_at = ranges[h][2]
            acc[at, :] = acc[at, :] + core_in[core_at : core_at + length[h], :]
        slots = {h: ranges[h][3] for h in parts}
        for step in range(bits):
            flying = []
            if with_small:
                small_copy = send_small(step + 1, across(step))
            for h in parts:
                bit = (step + h) % bits
                half = length[h] // 2
                mine = digit(bit)
                slot = slots[h]
                other = offset[h] + (1 - mine) * half
                out_buf[slot : slot + half, :] = acc[rows_at(other, half), :].astype(BF16)
                flying.append(
                    (
                        slot,
                        send(
                            out_buf.at[pl.ds(slot, half)], in_buf.at[pl.ds(slot, half)],
                            send_sem.at[h, step + 1], recv_sem.at[h, step + 1], across(bit),
                        ),
                    )
                )
                offset[h] = offset[h] + mine * half
                length[h] = half
                slots[h] = slot + half
            yield
            if with_small:
                add_small(step + 1, small_copy)
            for h, (place, copy) in zip(parts, flying):
                copy.wait_recv()
                at = rows_at(offset[h], length[h])
                value = acc[at, :] + in_buf[place : place + length[h], :].astype(F32)
                if step < bits - 1:
                    acc[at, :] = value
                else:
                    res[at, :] = value.astype(BF16)
        for step in range(bits + 1):
            flying = []
            for h in parts:
                last = step == bits
                bit = (bits - 1 - step + h) % bits
                mine = sub if last else digit(bit)
                at = rows_at(offset[h], length[h])
                sem = bits + 1 + step
                flying.append(
                    send(
                        res.at[at], res.at[at], send_sem.at[h, sem], recv_sem.at[h, sem],
                        core if last else across(bit),
                    )
                )
                offset[h] = offset[h] - mine * length[h]
                length[h] = 2 * length[h]
            yield
            for copy in flying:
                copy.wait_recv()

    for i in range(KSIZE * KSIZE):
        taps[i] = jnp.broadcast_to(dw_ref[i : i + 1, :], (8, width))
    dk[...] = jnp.zeros_like(dk)
    up_acc[...] = jnp.zeros_like(up_acc)
    down_acc[...] = jnp.zeros_like(down_acc)
    gres_all[...] = jnp.zeros_like(gres_all)
    acc[base_enc:, :] = jnp.zeros((acc.shape[0] - base_enc, width), F32)
    small_now[0] = jnp.zeros((8, width), F32)
    inside = lax.broadcasted_iota(jnp.int32, (LANES, width), 0) < groups * 8

    @pl.loop(0, wide)
    def _(r):
        enc = dot(x_ref[r], w_enc_ref[...], (0, 0)).astype(BF16).astype(F32)
        for b in range(KSIZE):
            moved = enc if b == 0 else pltpu.roll(enc, LANES - b, 0)
            shifted[b, r] = jnp.where(inside, moved, 0.0)

    conv[:, groups * 8 :, :] = jnp.zeros((rows, LANES - groups * 8, width), F32)

    def part_of(step):
        return (
            pl.ds(pl.multiple_of((step // lane_parts) * 8, 8), 8),
            pl.ds(pl.multiple_of((step % lane_parts) * LANES, LANES), LANES),
        )

    @pl.loop(0, groups * lane_parts)
    def _(step):
        at = part_of(step)
        total = jnp.zeros((rows, 8, LANES), F32)
        for b in range(KSIZE):
            line = shifted[(b, slice(None)) + at]
            for a in range(KSIZE):
                total = total + line[a : a + rows] * taps[a * KSIZE + b, :, at[1]][None]
        conv[(slice(None),) + at] = total

    gain = gain_ref[...]
    mask = jnp.concatenate([mask_ref[...]] * 2, axis=1)
    gscale = jnp.concatenate([gscale_ref[...]] * 2, axis=1)

    @pl.loop(0, rows // 2)
    def _(step):
        y = step * 2
        cv = conv[pl.ds(y, 2)].reshape(2 * LANES, width)
        centred = cv - jnp.mean(cv, axis=-1, keepdims=True)
        inv_std = lax.rsqrt(jnp.mean(centred * centred, axis=-1, keepdims=True) + 1e-06)
        normed = centred * inv_std
        scaled = (normed * gain).astype(BF16)
        pre = dot(scaled, w_up_ref[...], (1, 0))
        square = pre * pre
        th = jnp.tanh(GELU_C * (pre + GELU_A * (square * pre)))
        half = 0.5 * (1.0 + th)
        act = (pre * half).astype(BF16)
        slope = half + (0.5 * GELU_C) * pre * (1.0 - th * th) * (1.0 + (3.0 * GELU_A) * square)
        centre = shifted[RIM, pl.ds(y + RIM, 2)].reshape(2 * LANES, width)
        residual = (centre + dot(act, w_down_ref[...], (1, 0))).astype(BF16)
        readout = dot(w_dec_t_ref[...], residual, (1, 1))
        base = jnp.concatenate(
            [
                pltpu.roll(x_ref[y + RIM + i].astype(F32), LANES - RIM, 1)
                for i in range(2)
            ],
            axis=1,
        )
        goal = jnp.concatenate([goal_ref[y + i] for i in range(2)], axis=1).astype(F32)
        pred = base + readout
        keep = jnp.where(mask > 0.0, pred, base).astype(BF16)
        pred_ref[y] = keep[:, :LANES]
        pred_ref[y + 1] = keep[:, LANES:]
        misfit = (pred - goal) * mask
        small_now[0, 0:1, :] += jnp.sum(misfit * misfit, axis=0, keepdims=True)
        gout = (misfit * gscale).astype(BF16)
        acc[base_dec : base_dec + chan, :] += dot(gout, residual, (1, 0))
        gres = dot(gout, w_dec_t_ref[...], (0, 0)).astype(BF16)
        gres_all[pl.ds(y + RIM, 2)] = gres.astype(F32).reshape(2, LANES, width)
        down_acc[...] += dot(gres, act, (0, 0))
        gpre = (dot(gres, w_down_ref[...], (1, 1)) * slope).astype(BF16)
        up_acc[...] += dot(scaled, gpre, (0, 0))
        gscaled = dot(gpre, w_up_ref[...], (1, 1))
        small_now[0, 1:2, :] += jnp.sum(gscaled * normed, axis=0, keepdims=True)
        g = gscaled * gain
        gconv = inv_std * (
            g
            - jnp.mean(g, axis=-1, keepdims=True)
            - normed * jnp.mean(g * normed, axis=-1, keepdims=True)
        )
        conv[pl.ds(y, 2)] = gconv.reshape(2, LANES, width)

    for k in range(hid // width):
        cols = slice(k * width, (k + 1) * width)
        acc[cols, :] = up_acc[:, cols]
        acc[hid + k * width : hid + (k + 1) * width, :] = down_acc[:, cols].T

    pl.semaphore_wait(barrier, bits + 1)
    flow = exchange([0, 1], True)
    next(flow)

    def depthwise_back(step):
        at = part_of(step)
        gc = conv[(slice(None),) + at]
        gc_rows = [gc[y] for y in range(rows)]
        for b in range(KSIZE):
            line = shifted[(b, slice(None)) + at]
            for a in range(KSIZE):
                dk[a * KSIZE + b, :, at[1]] += jnp.sum(gc * line[a : a + rows], axis=0)
            spread = [None] * wide
            for a in range(KSIZE):
                tap = taps[a * KSIZE + b, :, at[1]]
                for y in range(rows):
                    term = gc_rows[y] * tap
                    old = spread[y + a]
                    spread[y + a] = term if old is None else old + term
            for r in range(wide):
                shifted[(b, r) + at] = spread[r]

    def encoder_back(r):
        g = pltpu.roll(gres_all[r], RIM, 0) + shifted[0, r]
        for b in range(1, KSIZE):
            g = g + pltpu.roll(shifted[b, r], b, 0)
        acc[base_enc : base_enc + chan, :] += dot(x_ref[r], g.astype(BF16), (1, 0))

    steps = groups * lane_parts
    for piece in range(3):
        pl.loop(piece * steps // 3, (piece + 1) * steps // 3)(depthwise_back)
        next(flow, None)
    pl.loop(0, wide)(encoder_back)
    for i in range(KSIZE * KSIZE):
        acc[base_dw + i : base_dw + i + 1, :] = jnp.sum(dk[i], axis=0, keepdims=True)
    tail = exchange([2], False)
    next(tail)
    for _ in range(bits + 1):
        next(flow, None)
        next(tail, None)
    for _ in flow:
        next(tail, None)
    small_out[...] = small_now[bits + 1]
    for k in range(hid // width):
        up_ref[:, k * width : (k + 1) * width] = res[k * width : (k + 1) * width, :]
    down_ref[...] = res[hid : 2 * hid, :]
    for _ in tail:
        pass
    enc_ref[...] = res[base_enc : base_enc + 80, :][:chan]
    dec_ref[...] = res[base_dec : base_dec + 80, :][:chan]
    dw_out[...] = res[base_dw : base_dw + 64, :][: dw_out.shape[0]]
    for copy in started:
        copy.wait_send()


def shards(state, target, tile_plan, w_enc, dw_kernel, norm_gain, w_up, w_down, w_dec):
    chan, rows, cols = state.shape
    width, hid = w_up.shape
    wide = rows + KSIZE - 1
    tile_cols = cols // PW
    band_at = lax.axis_index("band")
    sub_at = lax.axis_index("sub")
    before, after = with_halo(state, "sub", 2, RIM, True)
    fill = jnp.zeros((chan, rows, LANES - cols - 2 * RIM), BF16)
    lon = jnp.concatenate([before, state, after, fill], axis=2)
    above, below = with_halo(lon, "band", 1, RIM, False)
    x = jnp.concatenate([above, lon, below], axis=1).transpose(1, 0, 2)
    goal = jnp.pad(target.transpose(1, 0, 2), ((0, 0), (0, 0), (0, LANES - cols)))
    plan = lax.dynamic_slice(tile_plan, (band_at, sub_at * tile_cols), (1, tile_cols))
    wet = (plan >= 0).astype(F32)
    mask = jnp.pad(jnp.repeat(wet, PW, axis=1), ((0, 0), (0, LANES - cols)))
    inv_count = 1.0 / (jnp.sum((tile_plan >= 0).astype(F32)) * (chan * PW * PW))
    band_size = lax.axis_size("band")
    bits = band_size.bit_length() - 1
    unit = 32 * band_size
    cuts = [hid, hid, -(-(80 + 80 + 64) // unit) * unit]
    ranges = []
    base = staged = 0
    for size in cuts:
        ranges.append((base, size, base // 2, staged))
        base += size
        staged += sum(size // 2 // (1 << (s + 1)) for s in range(bits))
    vmem = pl.BlockSpec(memory_space=pltpu.VMEM)
    dma = pltpu.SemaphoreType.DMA
    pred, small, g_up, g_down, g_enc, g_dw, g_dec = pl.pallas_call(
        functools.partial(block_kernel, ranges, band_size),
        out_shape=(
            jax.ShapeDtypeStruct((rows, chan, LANES), BF16),
            jax.ShapeDtypeStruct((8, width), F32),
            jax.ShapeDtypeStruct((width, hid), BF16),
            jax.ShapeDtypeStruct((hid, width), BF16),
            jax.ShapeDtypeStruct((chan, width), BF16),
            jax.ShapeDtypeStruct((KSIZE * KSIZE, width), BF16),
            jax.ShapeDtypeStruct((chan, width), BF16),
        ),
        in_specs=[vmem] * 10,
        out_specs=(vmem,) * 7,
        scratch_shapes=[
            pltpu.VMEM((KSIZE, wide, LANES, width), F32),
            pltpu.VMEM((rows, LANES, width), F32),
            pltpu.VMEM((wide, LANES, width), F32),
            pltpu.VMEM((KSIZE * KSIZE, 8, width), F32),
            pltpu.VMEM((KSIZE * KSIZE, 8, width), F32),
            pltpu.VMEM((width, hid), F32),
            pltpu.VMEM((width, hid), F32),
            pltpu.VMEM((base, width), F32),
            pltpu.VMEM((base // 2, width), F32),
            pltpu.VMEM((staged, width), BF16),
            pltpu.VMEM((staged, width), BF16),
            pltpu.VMEM((base, width), BF16),
            pltpu.VMEM((bits + 2, 8, width), F32),
            pltpu.VMEM((bits + 1, 8, width), F32),
            dma((3, 2 * bits + 2)),
            dma((3, 2 * bits + 2)),
            dma((bits + 1,)),
            dma((bits + 1,)),
        ],
        compiler_params=pltpu.CompilerParams(
            collective_id=0, has_side_effects=True, vmem_limit_bytes=52 * 1024 * 1024
        ),
        name="block",
    )(
        x, goal, mask, mask * (2.0 * inv_count), w_enc, dw_kernel.astype(F32),
        norm_gain.reshape(1, width), w_up, w_down, w_dec.T,
    )
    new_field = pred[:, :, :cols].transpose(1, 0, 2)
    return (
        new_field,
        (jnp.sum(small[0]) * inv_count).reshape(1),
        g_enc.astype(F32),
        g_dw.astype(F32),
        small[1],
        g_up.astype(F32),
        g_down.astype(F32),
        g_dec.T.astype(F32),
    )


def solution(mesh):
    split = P("groups", "band", "sub")
    parts = P("groups", None)
    return jax.shard_map(
        shards,
        mesh=mesh,
        in_specs=(split, split, parts) + (P(),) * 6,
        out_specs=(split, P("groups"), parts, parts, P("groups"), parts, parts, parts),
        check_vma=False,
    )
```

```python
import functools
import math

import jax
import jax.numpy as jnp
from jax import lax
from jax.experimental import pallas as pl
from jax.experimental.pallas import tpu as pltpu
from jax.sharding import PartitionSpec as P

KSIZE = 7
RIM = 3
PW = 12
LANES = 128
F32 = jnp.float32
BF16 = jnp.bfloat16
GELU_C = math.sqrt(2.0 / math.pi)
GELU_A = 0.044715


def dot(left, right, dims):
    return lax.dot_general(left, right, ((dims[:1], dims[1:]), ((), ())), preferred_element_type=F32)


def rows_at(start, size):
    return pl.ds(pl.multiple_of(start, 16), size)


def block_kernel(
    ranges, band_size, x_ref, goal_ref, mask_ref, gscale_ref, w_enc_ref, dw_ref, gain_ref, w_up_ref,
    w_down_ref, w_dec_t_ref, pred_ref, small_out, up_ref, down_ref, enc_ref, dw_out, dec_ref,
    shifted, conv, gres_all, taps, dk, up_acc, down_acc, acc, core_in, out_buf, in_buf, res,
    small_now, small_in, send_sem, recv_sem, small_send, small_recv, x_all, x_other, edge, halo_send,
    halo_recv,
):
    chan = w_dec_t_ref.shape[0]
    deep = x_ref.shape[1]
    width = w_enc_ref.shape[1]
    hid = w_up_ref.shape[1]
    rows = goal_ref.shape[0]
    wide = rows + KSIZE - 1
    groups = (LANES - 8) // 8
    lane_parts = width // LANES
    base_enc = 2 * hid
    base_dec = base_enc + 80
    base_dw = base_dec + 80

    band = lax.axis_index("band")
    sub = lax.axis_index("sub")
    bits = band_size.bit_length() - 1
    core = {"band": band, "sub": 1 - sub}
    started = []

    def digit(bit):
        return (band // (1 << bit)) % 2

    def across(bit):
        return {"band": band + (1 - 2 * digit(bit)) * (1 << bit), "sub": sub}

    barrier = pltpu.get_barrier_semaphore()
    for peer in [core] + [across(bit) for bit in range(bits)]:
        pl.semaphore_signal(barrier, inc=1, device_id=peer, device_id_type=pl.DeviceIdType.MESH)

    extra = band - 1 + 2 * digit(0)
    has_extra = (extra >= 0) & (extra < band_size)

    @pl.when(has_extra)
    def _():
        pl.semaphore_signal(
            barrier, inc=1, device_id={"band": extra, "sub": sub},
            device_id_type=pl.DeviceIdType.MESH,
        )

    def send(src, dst, send_at, recv_at, peer):
        copy = pltpu.make_async_remote_copy(
            src_ref=src, dst_ref=dst, send_sem=send_at, recv_sem=recv_at,
            device_id=peer, device_id_type=pl.DeviceIdType.MESH,
        )
        copy.start()
        started.append(copy)
        return copy

    def send_small(step, peer):
        return send(
            small_now.at[step], small_in.at[step], small_send.at[step], small_recv.at[step], peer
        )

    def add_small(step, copy):
        copy.wait_recv()
        small_now[step + 1] = small_now[step] + small_in[step]

    def exchange(parts, with_small):
        small_copy = send_small(0, core) if with_small else None
        first = []
        offset = {}
        length = {}
        for h in parts:
            base, size, core_at, _ = ranges[h]
            half = size // 2
            first.append(
                send(
                    acc.at[rows_at(base + (1 - sub) * half, half)],
                    core_in.at[pl.ds(core_at, half)],
                    send_sem.at[h, 0], recv_sem.at[h, 0], core,
                )
            )
            offset[h] = base + sub * half
            length[h] = half
        yield
        if with_small:
            add_small(0, small_copy)
        for h, copy in zip(parts, first):
            copy.wait_recv()
            at = rows_at(offset[h], length[h])
            core_at = ranges[h][2]
            acc[at, :] = acc[at, :] + core_in[core_at : core_at + length[h], :]
        slots = {h: ranges[h][3] for h in parts}
        for step in range(bits):
            flying = []
            if with_small:
                small_copy = send_small(step + 1, across(step))
            for h in parts:
                bit = (step + h) % bits
                half = length[h] // 2
                mine = digit(bit)
                slot = slots[h]
                other = offset[h] + (1 - mine) * half
                out_buf[slot : slot + half, :] = acc[rows_at(other, half), :].astype(BF16)
                flying.append(
                    (
                        slot,
                        send(
                            out_buf.at[pl.ds(slot, half)], in_buf.at[pl.ds(slot, half)],
                            send_sem.at[h, step + 1], recv_sem.at[h, step + 1], across(bit),
                        ),
                    )
                )
                offset[h] = offset[h] + mine * half
                length[h] = half
                slots[h] = slot + half
            yield
            if with_small:
                add_small(step + 1, small_copy)
            for h, (place, copy) in zip(parts, flying):
                copy.wait_recv()
                at = rows_at(offset[h], length[h])
                value = acc[at, :] + in_buf[place : place + length[h], :].astype(F32)
                if step < bits - 1:
                    acc[at, :] = value
                else:
                    res[at, :] = value.astype(BF16)
        for step in range(bits + 1):
            flying = []
            for h in parts:
                last = step == bits
                bit = (bits - 1 - step + h) % bits
                mine = sub if last else digit(bit)
                at = rows_at(offset[h], length[h])
                sem = bits + 1 + step
                flying.append(
                    send(
                        res.at[at], res.at[at], send_sem.at[h, sem], recv_sem.at[h, sem],
                        core if last else across(bit),
                    )
                )
                offset[h] = offset[h] - mine * length[h]
                length[h] = 2 * length[h]
            yield
            for copy in flying:
                copy.wait_recv()

    for i in range(KSIZE * KSIZE):
        taps[i] = jnp.broadcast_to(dw_ref[i : i + 1, :], (8, width))
    dk[...] = jnp.zeros_like(dk)
    up_acc[...] = jnp.zeros_like(up_acc)
    down_acc[...] = jnp.zeros_like(down_acc)
    gres_all[...] = jnp.zeros_like(gres_all)
    acc[base_enc:, :] = jnp.zeros((acc.shape[0] - base_enc, width), F32)
    small_now[0] = jnp.zeros((8, width), F32)
    inside = lax.broadcasted_iota(jnp.int32, (LANES, width), 0) < groups * 8

    def northward():
        return pltpu.make_async_remote_copy(
            src_ref=x_ref.at[pl.ds(0, RIM)], dst_ref=edge.at[1],
            send_sem=halo_send.at[1], recv_sem=halo_recv.at[1],
            device_id={"band": (band + band_size - 1) % band_size, "sub": sub},
            device_id_type=pl.DeviceIdType.MESH,
        )

    def southward():
        return pltpu.make_async_remote_copy(
            src_ref=x_ref.at[pl.ds(rows - RIM, RIM)], dst_ref=edge.at[0],
            send_sem=halo_send.at[2], recv_sem=halo_recv.at[2],
            device_id={"band": (band + 1) % band_size, "sub": sub},
            device_id_type=pl.DeviceIdType.MESH,
        )

    has_north = band > 0
    has_south = band < band_size - 1
    pl.semaphore_wait(barrier, bits + 1 + has_extra.astype(jnp.int32))

    strip = send(x_ref, x_other.at[pl.ds(RIM, rows)], halo_send.at[0], halo_recv.at[0], core)

    @pl.when(has_north)
    def _():
        northward().start()

    @pl.when(has_south)
    def _():
        southward().start()

    lane = lax.broadcasted_iota(jnp.int32, (deep, LANES), 1)
    span = groups * 8

    def encode(own, other, r):
        far = other.astype(F32)
        left = pltpu.roll(far, LANES - span, 1)
        right = pltpu.roll(far, span, 1)
        near = jnp.where(lane < RIM, left, jnp.where(lane < span + RIM, own.astype(F32), right))
        cells = jnp.where(lane < span + 2 * RIM, near, 0.0).astype(BF16)
        x_all[r] = cells
        enc = dot(cells, w_enc_ref[...], (0, 0)).astype(BF16).astype(F32)
        for b in range(KSIZE):
            moved = enc if b == 0 else pltpu.roll(enc, LANES - b, 0)
            shifted[b, r] = jnp.where(inside, moved, 0.0)

    strip.wait_recv()

    @pl.loop(0, rows)
    def _(y):
        encode(x_ref[y], x_other[y + RIM], y + RIM)

    @pl.when(has_north)
    def _():
        southward().wait_recv()

    @pl.when(band == 0)
    def _():
        edge[0] = jnp.zeros((RIM, deep, LANES), BF16)

    @pl.when(has_south)
    def _():
        northward().wait_recv()

    @pl.when(band == band_size - 1)
    def _():
        edge[1] = jnp.zeros((RIM, deep, LANES), BF16)

    top = send(edge.at[0], x_other.at[pl.ds(0, RIM)], halo_send.at[3], halo_recv.at[3], core)
    bottom = send(
        edge.at[1], x_other.at[pl.ds(rows + RIM, RIM)], halo_send.at[4], halo_recv.at[4], core
    )
    top.wait_recv()
    bottom.wait_recv()

    @pl.loop(0, RIM)
    def _(k):
        encode(edge[0, k], x_other[k], k)
        encode(edge[1, k], x_other[rows + RIM + k], rows + RIM + k)

    conv[:, groups * 8 :, :] = jnp.zeros((rows, LANES - groups * 8, width), F32)

    def part_of(step):
        return (
            pl.ds(pl.multiple_of((step // lane_parts) * 8, 8), 8),
            pl.ds(pl.multiple_of((step % lane_parts) * LANES, LANES), LANES),
        )

    @pl.loop(0, groups * lane_parts)
    def _(step):
        at = part_of(step)
        total = jnp.zeros((rows, 8, LANES), F32)
        for b in range(KSIZE):
            line = shifted[(b, slice(None)) + at]
            for a in range(KSIZE):
                total = total + line[a : a + rows] * taps[a * KSIZE + b, :, at[1]][None]
        conv[(slice(None),) + at] = total

    gain = gain_ref[...]
    mask = jnp.concatenate([mask_ref[...]] * 2, axis=1)
    gscale = jnp.concatenate([gscale_ref[...]] * 2, axis=1)

    @pl.loop(0, rows // 2)
    def _(step):
        y = step * 2
        cv = conv[pl.ds(y, 2)].reshape(2 * LANES, width)
        centred = cv - jnp.mean(cv, axis=-1, keepdims=True)
        inv_std = lax.rsqrt(jnp.mean(centred * centred, axis=-1, keepdims=True) + 1e-06)
        normed = centred * inv_std
        scaled = (normed * gain).astype(BF16)
        pre = dot(scaled, w_up_ref[...], (1, 0))
        square = pre * pre
        th = jnp.tanh(GELU_C * (pre + GELU_A * (square * pre)))
        half = 0.5 * (1.0 + th)
        act = (pre * half).astype(BF16)
        slope = half + (0.5 * GELU_C) * pre * (1.0 - th * th) * (1.0 + (3.0 * GELU_A) * square)
        centre = shifted[RIM, pl.ds(y + RIM, 2)].reshape(2 * LANES, width)
        residual = (centre + dot(act, w_down_ref[...], (1, 0))).astype(BF16)
        readout = dot(w_dec_t_ref[...], residual, (1, 1))
        base = jnp.concatenate(
            [
                pltpu.roll(x_all[y + RIM + i].astype(F32), LANES - RIM, 1)[:chan]
                for i in range(2)
            ],
            axis=1,
        )
        goal = jnp.concatenate([goal_ref[y + i] for i in range(2)], axis=1).astype(F32)
        pred = base + readout
        keep = jnp.where(mask > 0.0, pred, base).astype(BF16)
        pred_ref[y] = keep[:, :LANES]
        pred_ref[y + 1] = keep[:, LANES:]
        misfit = (pred - goal) * mask
        small_now[0, 0:1, :] += jnp.sum(misfit * misfit, axis=0, keepdims=True)
        gout = (misfit * gscale).astype(BF16)
        acc[base_dec : base_dec + chan, :] += dot(gout, residual, (1, 0))
        gres = dot(gout, w_dec_t_ref[...], (0, 0)).astype(BF16)
        gres_all[pl.ds(y + RIM, 2)] = gres.astype(F32).reshape(2, LANES, width)
        down_acc[...] += dot(gres, act, (0, 0))
        gpre = (dot(gres, w_down_ref[...], (1, 1)) * slope).astype(BF16)
        up_acc[...] += dot(scaled, gpre, (0, 0))
        gscaled = dot(gpre, w_up_ref[...], (1, 1))
        small_now[0, 1:2, :] += jnp.sum(gscaled * normed, axis=0, keepdims=True)
        g = gscaled * gain
        gconv = inv_std * (
            g
            - jnp.mean(g, axis=-1, keepdims=True)
            - normed * jnp.mean(g * normed, axis=-1, keepdims=True)
        )
        conv[pl.ds(y, 2)] = gconv.reshape(2, LANES, width)

    for k in range(hid // width):
        cols = slice(k * width, (k + 1) * width)
        acc[cols, :] = up_acc[:, cols]
        acc[hid + k * width : hid + (k + 1) * width, :] = down_acc[:, cols].T

    flow = exchange([0, 1], True)
    next(flow)

    def depthwise_back(step):
        at = part_of(step)
        gc = conv[(slice(None),) + at]
        gc_rows = [gc[y] for y in range(rows)]
        for b in range(KSIZE):
            line = shifted[(b, slice(None)) + at]
            for a in range(KSIZE):
                dk[a * KSIZE + b, :, at[1]] += jnp.sum(gc * line[a : a + rows], axis=0)
            spread = [None] * wide
            for a in range(KSIZE):
                tap = taps[a * KSIZE + b, :, at[1]]
                for y in range(rows):
                    term = gc_rows[y] * tap
                    old = spread[y + a]
                    spread[y + a] = term if old is None else old + term
            for r in range(wide):
                shifted[(b, r) + at] = spread[r]

    def encoder_back(r):
        g = pltpu.roll(gres_all[r], RIM, 0) + shifted[0, r]
        for b in range(1, KSIZE):
            g = g + pltpu.roll(shifted[b, r], b, 0)
        acc[base_enc : base_enc + deep, :] += dot(x_all[r], g.astype(BF16), (1, 0))

    steps = groups * lane_parts
    for piece in range(3):
        pl.loop(piece * steps // 3, (piece + 1) * steps // 3)(depthwise_back)
        next(flow, None)
    pl.loop(0, wide)(encoder_back)
    for i in range(KSIZE * KSIZE):
        acc[base_dw + i : base_dw + i + 1, :] = jnp.sum(dk[i], axis=0, keepdims=True)
    tail = exchange([2], False)
    next(tail)
    for _ in range(bits + 1):
        next(flow, None)
        next(tail, None)
    for _ in flow:
        next(tail, None)
    small_out[...] = small_now[bits + 1]
    for k in range(hid // width):
        up_ref[:, k * width : (k + 1) * width] = res[k * width : (k + 1) * width, :]
    down_ref[...] = res[hid : 2 * hid, :]
    for _ in tail:
        pass
    enc_ref[...] = res[base_enc : base_enc + 80, :][:chan]
    dec_ref[...] = res[base_dec : base_dec + 80, :][:chan]
    dw_out[...] = res[base_dw : base_dw + 64, :][: dw_out.shape[0]]
    for copy in started:
        copy.wait_send()

    @pl.when(has_north)
    def _():
        northward().wait_send()

    @pl.when(has_south)
    def _():
        southward().wait_send()


def shards(state, target, tile_plan, w_enc, dw_kernel, norm_gain, w_up, w_down, w_dec):
    chan, rows, cols = state.shape
    width, hid = w_up.shape
    wide = rows + KSIZE - 1
    tile_cols = cols // PW
    band_at = lax.axis_index("band")
    sub_at = lax.axis_index("sub")
    deep = -(-chan // 16) * 16
    x = jnp.pad(
        state.transpose(1, 0, 2), ((0, 0), (0, deep - chan), (RIM, LANES - cols - RIM))
    )
    w_in = jnp.pad(w_enc, ((0, deep - chan), (0, 0)))
    goal = jnp.pad(target.transpose(1, 0, 2), ((0, 0), (0, 0), (0, LANES - cols)))
    plan = lax.dynamic_slice(tile_plan, (band_at, sub_at * tile_cols), (1, tile_cols))
    wet = (plan >= 0).astype(F32)
    mask = jnp.pad(jnp.repeat(wet, PW, axis=1), ((0, 0), (0, LANES - cols)))
    inv_count = 1.0 / (jnp.sum((tile_plan >= 0).astype(F32)) * (chan * PW * PW))
    band_size = lax.axis_size("band")
    bits = band_size.bit_length() - 1
    unit = 32 * band_size
    cuts = [hid, hid, -(-(80 + 80 + 64) // unit) * unit]
    ranges = []
    base = staged = 0
    for size in cuts:
        ranges.append((base, size, base // 2, staged))
        base += size
        staged += sum(size // 2 // (1 << (s + 1)) for s in range(bits))
    vmem = pl.BlockSpec(memory_space=pltpu.VMEM)
    dma = pltpu.SemaphoreType.DMA
    pred, small, g_up, g_down, g_enc, g_dw, g_dec = pl.pallas_call(
        functools.partial(block_kernel, ranges, band_size),
        out_shape=(
            jax.ShapeDtypeStruct((rows, chan, LANES), BF16),
            jax.ShapeDtypeStruct((8, width), F32),
            jax.ShapeDtypeStruct((width, hid), BF16),
            jax.ShapeDtypeStruct((hid, width), BF16),
            jax.ShapeDtypeStruct((chan, width), BF16),
            jax.ShapeDtypeStruct((KSIZE * KSIZE, width), BF16),
            jax.ShapeDtypeStruct((chan, width), BF16),
        ),
        in_specs=[vmem] * 10,
        out_specs=(vmem,) * 7,
        scratch_shapes=[
            pltpu.VMEM((KSIZE, wide, LANES, width), F32),
            pltpu.VMEM((rows, LANES, width), F32),
            pltpu.VMEM((wide, LANES, width), F32),
            pltpu.VMEM((KSIZE * KSIZE, 8, width), F32),
            pltpu.VMEM((KSIZE * KSIZE, 8, width), F32),
            pltpu.VMEM((width, hid), F32),
            pltpu.VMEM((width, hid), F32),
            pltpu.VMEM((base, width), F32),
            pltpu.VMEM((base // 2, width), F32),
            pltpu.VMEM((staged, width), BF16),
            pltpu.VMEM((staged, width), BF16),
            pltpu.VMEM((base, width), BF16),
            pltpu.VMEM((bits + 2, 8, width), F32),
            pltpu.VMEM((bits + 1, 8, width), F32),
            dma((3, 2 * bits + 2)),
            dma((3, 2 * bits + 2)),
            dma((bits + 1,)),
            dma((bits + 1,)),
            pltpu.VMEM((wide, deep, LANES), BF16),
            pltpu.VMEM((wide, deep, LANES), BF16),
            pltpu.VMEM((2, RIM, deep, LANES), BF16),
            dma((5,)),
            dma((5,)),
        ],
        compiler_params=pltpu.CompilerParams(
            collective_id=0, has_side_effects=True, vmem_limit_bytes=52 * 1024 * 1024
        ),
        name="block",
    )(
        x, goal, mask, mask * (2.0 * inv_count), w_in, dw_kernel.astype(F32),
        norm_gain.reshape(1, width), w_up, w_down, w_dec.T,
    )
    new_field = pred[:, :, :cols].transpose(1, 0, 2)
    return (
        new_field,
        (jnp.sum(small[0]) * inv_count).reshape(1),
        g_enc.astype(F32),
        g_dw.astype(F32),
        small[1],
        g_up.astype(F32),
        g_down.astype(F32),
        g_dec.T.astype(F32),
    )


def solution(mesh):
    split = P("groups", "band", "sub")
    parts = P("groups", None)
    return jax.shard_map(
        shards,
        mesh=mesh,
        in_specs=(split, split, parts) + (P(),) * 6,
        out_specs=(split, P("groups"), parts, parts, P("groups"), parts, parts, parts),
        check_vma=False,
    )
```
